32 devices in a mesh: mapx: 4 (over x, core), mapy: 4 (over z), layer: 2 (over y).
Axes of the slice: x: 2, y: 2, z: 4, core: 2. Of those that a mesh axis runs over, the one named last changes fastest.
Arguments:
- velocity: float32 [16, 2, 4, 32, 512], P(None, None, 'layer', 'mapx', 'mapy'), may hold values from -6 to 6
- viscosity: float32 [4, 32, 512], P('layer', 'mapx', 'mapy'), may hold values from 0.5 to 5
- friction: float32 [32, 512], P('mapx', 'mapy'), may hold values from 0.05 to 0.5
- owner: int32 [4, 4, 1024, 1], P('mapx', 'mapy'), may hold values from 0 to 7; in each aligned block of 1024 rows (0 to 1023, 1024 to 2047, ..., all dimensions but the last counted through in order) at most 256 rows name the same one
- cell: int32 [4, 4, 1024], P('mapx', 'mapy'), may hold values from 0 to 511
- directions: float32 [16, 16, 1024], P(None, 'mapx', ('mapy', 'layer')), may hold values from -6 to 6
- stiffness: float32 [16, 1024], P('mapx', ('mapy', 'layer')), may hold values from 0.02 to 0.2
Outputs:
- image: float32 [16, 2, 4, 32, 512], P(None, None, 'layer', 'mapx', 'mapy')
- hessian: float32 [16, 16, 1024], P(None, 'mapx', ('mapy', 'layer'))
The draws below stay inside these ranges and needn't reach their ends.
Inputs may be any that keep to these rules, and one draw needn't show every extreme that they name: Among the faces of one mesh block (aligned blocks of 1024 rows) no owner is named more than 256 times, a bound that some block reaches.
All inputs are finite; a program needn't handle non-finite values.
Results may differ from the reference program's by a relative error of at most 0.00002.
Values sent between devices are 32-bit elements; how exact they have to be, the bound alone decides.
A program may use at most 64 MiB of HBM per device.

```python
import math
import jax
import jax.numpy as jnp
import numpy as np
from jax import lax

PROBES = 16
CX = 8
CY = 128
MXD = 4
MYD = 128
NX = 32
NY = 512
NZ = 4
FACES = 1024
OWNERS = 8
CAP = 256
M_DEV = 512
MX = 16
MY = 1024
N_MAPX = 4
N_MAPY = 4


def place_ends(entries, key, least, high):
    extent = entries.shape
    index_at = [jax.random.randint(jax.random.fold_in(key, axis), (), 0, extent[axis]) for axis in range(len(extent))]
    entries = entries.at[tuple(index_at)].set(least)
    longest = extent.index(max(extent))
    index_at[longest] = (index_at[longest] + 1) % extent[longest]
    return entries.at[tuple(index_at)].set(high)


def shard_levels(own_key, dims, split, low, top_value):
    level = 1.0
    for axis_at, blocks in split:
        draws = jax.random.uniform(jax.random.fold_in(jax.random.fold_in(own_key, 6), axis_at), (blocks,), jnp.float32, low / len(split), top_value / len(split))
        level = level * jnp.repeat(jnp.exp(draws), dims[axis_at] // blocks).reshape((-1,) + (1,) * (len(dims) - 1 - axis_at))
    return level


def shared_out(rng, own, number, rows, amount, top, limit, skew):
    ranking = jax.random.permutation(rng, amount)
    crowded, ordinary = portions_of(amount, rows * top, limit, skew, True), portions_of(amount, rows * top, limit, skew, False)
    places = jnp.arange(amount)

    def named(lengths, rotation):
        used = int((lengths > 0).sum())
        fixed = max(1, used // 4)
        passed = fixed + (places - fixed + rotation * (used - fixed)) % max(1, amount - fixed)
        return jnp.zeros((amount,), jnp.int32).at[ranking[jnp.where(places < fixed, places, passed)]].set(jnp.asarray(lengths, jnp.int32))

    lengths = jnp.where(number % 4 == 0, named(crowded, number // 4), named(ordinary, number - number // 4 - 1))
    mixed = jax.random.permutation(jax.random.fold_in(own, 3), amount)
    source_of, receiver = mixed[0:amount // 2 * 2:2], mixed[1:amount // 2 * 2:2]
    room = jnp.minimum(lengths[source_of] - 1, limit - lengths[receiver]) // 2
    room = jnp.where((source_of == ranking[0]) | (receiver == ranking[0]) | (lengths[receiver] == 0), 0, jnp.maximum(room, 0))
    passed = jax.random.randint(jax.random.fold_in(own, 4), (amount // 2,), 0, 1 << 20) % (room + 1)
    lengths = lengths.at[source_of].add(-passed).at[receiver].add(passed)
    items = jnp.searchsorted(jnp.cumsum(lengths), jnp.arange(rows * top), side="right").astype(jnp.int32)
    grid = items.reshape(top, rows).T
    grid = grid[jax.random.permutation(jax.random.fold_in(own, 1), rows)]
    rotation = jax.random.randint(jax.random.fold_in(own, 2), (rows, 1), 0, top)
    return jnp.take_along_axis(grid, (jnp.arange(top)[None, :] + rotation) % top, axis=1)


def portions_of(amount, total, bound, slope, full):
    weights = [(1 << 20) // math.isqrt(rank ** slope) + 1 for rank in range(1, amount + 1)]
    largest = bound if full else min(bound, max(-(-total // amount), total * weights[0] // sum(weights)))
    least = 1 if total - largest >= amount - 1 else 0
    holding, spare = [largest] + [least] * (amount - 1), total - largest - least * (amount - 1)
    while spare > 0:
        candidates = [i for i in range(1, amount) if holding[i] < largest] or [i for i in range(1, amount) if holding[i] < bound]
        pool, budget = sum([weights[i] for i in candidates]), spare
        for i in candidates:
            addition = min(bound - holding[i], max(1, budget * weights[i] // pool), spare)
            holding[i] = holding[i] + addition
            spare = spare - addition
    return np.array(holding)


def scatter_about(own_key, shape, deviation, reach, shards=(), kind=jnp.bfloat16):
    level = shard_levels(own_key, shape, shards, -0.22, 0.18) if shards else 1.0
    result = jax.random.normal(own_key, shape, jnp.float32) * deviation * level
    return jnp.minimum(jnp.maximum(result, -reach), reach).astype(kind)


def setup_inputs(seed: int = 0) -> dict:
    splits = jax.random.split(jax.random.key(seed), 8)
    velocity = scatter_about(splits[0], (PROBES, 2, NZ, NX, NY), 1.0, 6.0, ((2, 2), (3, 4), (4, 4)), jnp.float32)
    viscosity = jnp.clip(jnp.exp(math.log(5.0) - 2.3025851 * jax.random.uniform(splits[1], (NZ, NX, NY), jnp.float32) ** shard_levels(splits[1], (NZ, NX, NY), ((0, 2), (1, 4), (2, 4)), -0.2, 0.2)), 0.5, 5.0)
    friction = jnp.clip(jnp.exp(math.log(0.5) - 2.3025851 * jax.random.uniform(splits[2], (NX, NY), jnp.float32) ** shard_levels(splits[2], (NX, NY), ((0, 4), (1, 4)), -0.2, 0.2)), 0.05, 0.5)
    owner_keys = jax.random.split(jax.random.fold_in(splits[3], 1), N_MAPX * N_MAPY * FACES // FACES)
    owner_turns = jax.random.permutation(jax.random.fold_in(splits[3], 3), N_MAPX * N_MAPY * FACES // FACES)
    owner = jax.vmap(lambda own, number: shared_out(jax.random.fold_in(splits[3], 2), own, number, FACES, OWNERS, 1, CAP, 2))(owner_keys, owner_turns).reshape((N_MAPX, N_MAPY, FACES, 1))
    cell = place_ends(jax.random.randint(splits[4], (N_MAPX, N_MAPY, FACES), 0, M_DEV), jax.random.fold_in(splits[4], 1), 0, M_DEV - 1).astype(jnp.int32)
    directions = scatter_about(splits[5], (PROBES, MX, MY), 1.0, 6.0, ((1, 4), (2, 8)), jnp.float32)
    stiffness = jnp.clip(jnp.exp(math.log(0.2) - 2.3025851 * jax.random.uniform(splits[6], (MX, MY), jnp.float32) ** shard_levels(splits[6], (MX, MY), ((0, 4), (1, 8)), -0.2, 0.2)), 0.02, 0.2)
    return dict(velocity=velocity, viscosity=viscosity, friction=friction, owner=owner, cell=cell, directions=directions, stiffness=stiffness)


def stencil(padded, viscous):
    center = padded[..., 1:-1, 1:-1, 1:-1]
    visc = viscous[1:-1, 1:-1, 1:-1]
    weight_x = jnp.array([1.0, 0.25], jnp.float32)[:, None, None, None]
    weight_y = jnp.array([0.25, 1.0], jnp.float32)[:, None, None, None]
    total = 2.0 * 0.5 * (visc + viscous[2:, 1:-1, 1:-1]) * (center - padded[..., 2:, 1:-1, 1:-1])
    total = total + 2.0 * 0.5 * (visc + viscous[:-2, 1:-1, 1:-1]) * (center - padded[..., :-2, 1:-1, 1:-1])
    total = total + weight_x * 0.5 * (visc + viscous[1:-1, 2:, 1:-1]) * (center - padded[..., 1:-1, 2:, 1:-1])
    total = total + weight_x * 0.5 * (visc + viscous[1:-1, :-2, 1:-1]) * (center - padded[..., 1:-1, :-2, 1:-1])
    total = total + weight_y * 0.5 * (visc + viscous[1:-1, 1:-1, 2:]) * (center - padded[..., 1:-1, 1:-1, 2:])
    total = total + weight_y * 0.5 * (visc + viscous[1:-1, 1:-1, :-2]) * (center - padded[..., 1:-1, 1:-1, :-2])
    return total


def laplace(padded):
    return 4.0 * padded[..., 1:-1, 1:-1] - padded[..., 2:, 1:-1] - padded[..., :-2, 1:-1] - padded[..., 1:-1, 2:] - padded[..., 1:-1, :-2]


def pad_map(field):
    return jnp.pad(field, ((0, 0), (1, 1), (1, 1)))


def reference(velocity, viscosity, friction, owner, cell, directions, stiffness):
    viscous = jnp.pad(viscosity, 1)

    def one_probe(field):
        return stencil(jnp.pad(field, ((0, 0), (1, 1), (1, 1), (1, 1))), viscous)

    image = lax.map(one_probe, velocity)
    trace = friction * (image[:, 0, 0] + image[:, 1, 0])
    probes = trace.shape[0]
    blocked = trace.reshape(probes, N_MAPX, CX, N_MAPY, CY).transpose(0, 1, 3, 2, 4)
    blocked = blocked.reshape(probes, N_MAPX, N_MAPY * FACES)
    target = owner[..., 0].reshape(N_MAPX, N_MAPY * FACES)
    local = cell.reshape(N_MAPX, N_MAPY * FACES)
    map_row = local // MYD
    map_col = target * MYD + local % MYD
    block_index = jnp.broadcast_to(jnp.arange(N_MAPX, dtype=jnp.int32)[:, None], map_row.shape)
    data = jnp.zeros((probes, N_MAPX, MXD, MY), jnp.float32)
    data = data.at[:, block_index, map_row, map_col].add(blocked)
    data = data.reshape(probes, MX, MY)
    inner = stiffness[None] * laplace(pad_map(directions))
    prior = laplace(pad_map(inner)) + 0.1 * directions
    return image, data + prior
```

```python
import functools

import jax
import jax.numpy as jnp
from jax import lax
from jax.experimental import pallas as pl
from jax.experimental.pallas import tpu as pltpu
from jax.sharding import PartitionSpec as P

F32 = jnp.float32
BF16 = jnp.bfloat16
X, Y, ZV, ZM, R, C = 0, 2, 4, 6, 8, 10


def corner_slot(dx, do):
    return (dx + 1) * 2 + (0 if do < 0 else 1)


def kernel(
    counts, vel, visc, fric, own, cell, dirs, stiff, img, hess,
    xs, xh, ys, yh, zh, mh, cs, ch, rs, rh, tr, onehot, lhs, part, got, prior,
    send, recv, part_send, part_recv,
):
    nx, ny, nl = counts
    no = ny * nl
    nq, depth, rows, cols = vel.shape
    nv = nq * depth
    probes = nq // 2
    mrows, mcols = stiff.shape
    halves = probes // 8
    ix, iy, il = lax.axis_index("mapx"), lax.axis_index("mapy"), lax.axis_index("layer")
    me = iy * nl + il

    def place(at_x, owner):
        return (at_x, lax.div(owner, nl), lax.rem(owner, nl))

    low_x, high_x = ix > 0, ix < nx - 1
    low_y, high_y = iy > 0, iy < ny - 1
    low_l, high_l = il > 0, il < nl - 1
    low_o, high_o = me > 0, me < no - 1

    def has(dx, do):
        good_x = {-1: low_x, 1: high_x}.get(dx)
        good_o = {-1: low_o, 1: high_o}.get(do)
        if good_x is None:
            return good_o
        return good_x if good_o is None else jnp.logical_and(good_x, good_o)

    barrier = pltpu.get_barrier_semaphore()
    for step in range(1, no):
        other = lax.rem(me + step, no)
        pl.semaphore_signal(
            barrier, inc=1, device_id=place(ix, other), device_id_type=pl.DeviceIdType.MESH
        )
    greeted = no - 1
    for dx in (-1, 1):
        for do in (-1, 0, 1):
            near = has(dx, do)
            greeted = greeted + near.astype(jnp.int32)

            @pl.when(near)
            def _(dx=dx, do=do):
                pl.semaphore_signal(
                    barrier, inc=1, device_id=place(ix + dx, me + do),
                    device_id_type=pl.DeviceIdType.MESH,
                )

    def remote(src, dst, out_sem, in_sem, device):
        return pltpu.make_async_remote_copy(
            src_ref=src, dst_ref=dst, send_sem=out_sem, recv_sem=in_sem,
            device_id=device, device_id_type=pl.DeviceIdType.MESH,
        )

    def pair(kind, src, dst, side, device):
        return remote(src, dst, send.at[kind + side], recv.at[kind + 1 - side], device)

    def x_copy(side):
        return pair(X, xs.at[side], xh.at[1 - side], side, place(ix + 2 * side - 1, me))

    def r_copy(side):
        return pair(R, rs.at[side], rh.at[1 - side], side, place(ix + 2 * side - 1, me))

    def y_copy(side):
        return pair(Y, ys.at[side], yh.at[1 - side], side, (ix, iy + 2 * side - 1, il))

    def z_copy(side):
        z = 0 if side == 0 else depth - 1
        return pair(ZV, vel.at[:, z], zh.at[1 - side], side, (ix, iy, il + 2 * side - 1))

    def m_copy(side):
        z = 0 if side == 0 else depth - 1
        return pair(ZM, visc.at[z], mh.at[1 - side], side, (ix, iy, il + 2 * side - 1))

    def c_copy(dx, do):
        return remote(
            cs.at[0 if do < 0 else 1], ch.at[corner_slot(-dx, -do)],
            send.at[C + corner_slot(dx, do)], recv.at[C + corner_slot(-dx, -do)],
            place(ix + dx, me + do),
        )

    lane = lax.broadcasted_iota(jnp.int32, (rows, cols), 1)
    sub = lax.broadcasted_iota(jnp.int32, (rows, cols), 0)
    zeros = jnp.zeros((rows, cols), F32)

    for z in range(depth):
        xs[0, z * nq:(z + 1) * nq, :] = vel[:, z, 0, :]
        xs[1, z * nq:(z + 1) * nq, :] = vel[:, z, rows - 1, :]
    for side, row in ((0, 0), (1, rows - 1)):
        xs[side, nv:nv + 8, :] = jnp.concatenate(
            [visc[z, row:row + 1, :] for z in range(depth)]
            + [jnp.zeros((8 - depth, cols), F32)], 0,
        )

    def put(value, at, packed):
        here = lane == at
        return (
            jnp.where(here, pltpu.roll(value, at, 1), packed[0]),
            jnp.where(here, pltpu.roll(value, at + 1, 1), packed[1]),
        )

    def pack_y(q, packed):
        for z in range(depth):
            packed = put(vel[q, z], z * nq + q, packed)
        return packed

    packed = lax.fori_loop(0, nq, pack_y, (zeros, zeros), unroll=8)
    for z in range(depth):
        packed = put(visc[z], nv + z, packed)
    ys[0], ys[1] = packed

    block = [dirs[pl.ds(r, probes, stride=mrows), :] for r in range(mrows)]
    rim = jnp.concatenate([stiff[...], jnp.zeros((8 - mrows, mcols), F32)], 0)
    for side, first in ((0, 0), (1, mrows - 2)):
        for r in range(2):
            rs[side, r * probes:(r + 1) * probes, :] = block[first + r]
        rs[side, 2 * probes:2 * probes + 8, :] = rim
        cs[side, 8:16, :] = rim
    two = lax.div(lane, 2)
    packed = (zeros, zeros)
    for k in range(mrows * halves):
        value = block[k // halves][(k % halves) * 8:(k % halves) * 8 + 8]
        packed = (
            jnp.where(two == k, pltpu.roll(value, 2 * k, 1) if k else value, packed[0]),
            jnp.where(two == k, pltpu.roll(value, 2 * k + 2, 1), packed[1]),
        )
    cs[0, 0:8, :], cs[1, 0:8, :] = packed

    pl.semaphore_wait(barrier, greeted)

    def when_near(near, copy):
        @pl.when(near)
        def _():
            copy().start()

    sides = (0, 1)
    near_x, near_y, near_l = (low_x, high_x), (low_y, high_y), (low_l, high_l)
    corners = [(dx, do) for dx in (-1, 0, 1) for do in (-1, 1)]
    for s in sides:
        when_near(near_x[s], functools.partial(x_copy, s))
        when_near(near_y[s], functools.partial(y_copy, s))
    for s in sides:
        when_near(near_l[s], functools.partial(m_copy, s))
        when_near(near_l[s], functools.partial(z_copy, s))
    for s in sides:
        when_near(near_x[s], functools.partial(r_copy, s))
    for dx, do in corners:
        when_near(has(dx, do), functools.partial(c_copy, dx, do))

    def zero_unless(near, ref, at):
        @pl.when(jnp.logical_not(near))
        def _():
            ref[at] = jnp.zeros(ref.shape[1:], F32)

    for s in sides:
        zero_unless(near_x[s], xh, s)
        zero_unless(near_y[s], yh, s)
        zero_unless(near_l[s], zh, s)
        zero_unless(near_l[s], mh, s)
        zero_unless(near_x[s], rh, s)
    for dx, do in corners:
        zero_unless(has(dx, do), ch, corner_slot(dx, do))

    span = 2 * mcols
    pairs = mrows // 2
    cells = cell[...]
    low = lax.rem(cells, span)
    group = own[...] * pairs + lax.div(cells, span)
    number = lax.broadcasted_iota(jnp.int32, (span, cols), 0)
    for x in range(rows):
        onehot[:, x * cols:(x + 1) * cols] = jnp.where(
            number == low[x:x + 1, :], 1.0, 0.0
        ).astype(BF16)

    def arrive(near, copy):
        @pl.when(near)
        def _():
            copy().wait_recv()

    def beside(value, index, halo_rows, halo_lanes):
        down = jnp.where(sub == 0, halo_rows[0], pltpu.roll(value, 1, 0))
        up = jnp.where(sub == rows - 1, halo_rows[1], pltpu.roll(value, rows - 1, 0))
        left = jnp.where(
            lane == 0, pltpu.roll(halo_lanes[0], cols - index, 1), pltpu.roll(value, 1, 1)
        )
        right = jnp.where(
            lane == cols - 1,
            pltpu.roll(halo_lanes[1], cols - 1 - index, 1),
            pltpu.roll(value, cols - 1, 1),
        )
        return down, up, left, right

    def rows_at(index):
        return tuple(
            jnp.broadcast_to(xh[s, pl.ds(index, 1), :], (rows, cols)) for s in sides
        )

    def plane(z, trace):
        lanes = (yh[0], yh[1])
        here = visc[z]
        around = beside(here, nv + z, rows_at(nv + z), lanes)
        mean = [0.5 * (here + other) for other in around]
        down_z = here + (mh[0] if z == 0 else visc[z - 1])
        up_z = here + (mh[1] if z == depth - 1 else visc[z + 1])
        weights = (
            (mean[0], mean[1], 0.25 * mean[2], 0.25 * mean[3]),
            (0.25 * mean[0], 0.25 * mean[1], mean[2], mean[3]),
        )
        rub = fric[...]

        def probe(p, carry):
            both = None
            for c in range(2):
                q = p * 2 + c
                value = vel[q, z]
                below = zh[0, q] if z == 0 else vel[q, z - 1]
                above = zh[1, q] if z == depth - 1 else vel[q, z + 1]
                index = z * nq + q
                total = up_z * (value - above) + down_z * (value - below)
                for weight, other in zip(
                    weights[c], beside(value, index, rows_at(index), lanes)
                ):
                    total = total + weight * (value - other)
                img[q, z] = total
                both = total if both is None else both + total
            if trace:
                tr[pl.ds(p, rows, stride=probes), :] = rub * both
            return carry

        lax.fori_loop(0, probes, probe, 0, unroll=4)

    for s in sides:
        arrive(near_x[s], functools.partial(x_copy, 1 - s))
        arrive(near_y[s], functools.partial(y_copy, 1 - s))

    chunk = min(8, no)
    tall = 2 * probes

    def part_copy(owner):
        return remote(
            part.at[owner], got.at[iy], part_send.at[owner], part_recv.at[iy], place(ix, owner)
        )

    @pl.when(il == 0)
    def _():
        plane(0, True)
        coarse, fine = [], []
        for x in range(rows):
            values = tr[x * probes:(x + 1) * probes, :]
            coarse.append(values.astype(BF16).astype(F32))
            fine.append(values - coarse[-1])

        def owners(base):
            for g in range(chunk * pairs):
                for x in range(rows):
                    mine = group[x:x + 1, :] == base * pairs + g
                    lhs[g * tall:(g + 1) * tall, x * cols:(x + 1) * cols] = jnp.concatenate(
                        [jnp.where(mine, coarse[x], 0.0), jnp.where(mine, fine[x], 0.0)], 0
                    ).astype(BF16)
            sums = lax.dot_general(
                lhs[...], onehot[...], (((1,), (1,)), ((), ())), preferred_element_type=F32
            )
            for j in range(chunk):
                for h in range(pairs):
                    at = (j * pairs + h) * tall
                    both = sums[at:at + probes] + sums[at + probes:at + tall]
                    for k in range(2):
                        row = (2 * h + k) * probes
                        part[base + j, row:row + probes, :] = both[:, k * mcols:(k + 1) * mcols]
            for j in range(chunk):
                @pl.when(base + j != me)
                def _(j=j):
                    part_copy(base + j).start()

        if no == chunk:
            owners(0)
        else:
            def step(i, carry):
                owners(i * chunk)
                return carry

            lax.fori_loop(0, no // chunk, step, 0)

    for s in sides:
        arrive(near_x[s], functools.partial(r_copy, 1 - s))
    for dx, do in corners:
        arrive(has(dx, do), functools.partial(c_copy, -dx, -do))

    def edge(dx, r):
        left, right = ch[corner_slot(dx, -1), 0:8, :], ch[corner_slot(dx, 1), 0:8, :]
        halfs = []
        for h in range(halves):
            k = 2 * (r * halves + h)
            from_right = pltpu.roll(right, mcols - k, 1) if k else right
            from_left = pltpu.roll(left, mcols - 2 - k, 1)
            halfs.append(
                jnp.where(lane < 2, from_right, jnp.where(lane >= mcols - 2, from_left, 0.0))
            )
        return jnp.concatenate(halfs, 0)

    wide = {}
    for r in range(2):
        wide[r - 2] = jnp.concatenate(
            [rh[0, r * probes:(r + 1) * probes, :], edge(-1, mrows - 2 + r)], 1
        )
        wide[mrows + r] = jnp.concatenate(
            [rh[1, r * probes:(r + 1) * probes, :], edge(1, r)], 1
        )
    for r in range(mrows):
        wide[r] = jnp.concatenate([dirs[pl.ds(r, probes, stride=mrows), :], edge(0, r)], 1)

    def laplace(field, r):
        return (
            4.0 * field[r] - field[r - 1] - field[r + 1]
            - pltpu.roll(field[r], 1, 1) - pltpu.roll(field[r], 2 * mcols - 1, 1)
        )

    line = lax.broadcasted_iota(jnp.int32, (1, mcols), 1)
    inner = {}
    for r in range(-1, mrows + 1):
        if r < 0:
            soft = rh[0, 2 * probes + mrows - 1:2 * probes + mrows, :]
        elif r == mrows:
            soft = rh[1, 2 * probes:2 * probes + 1, :]
        else:
            soft = stiff[r:r + 1, :]
        outer = jnp.zeros((1, mcols), F32)
        if 0 <= r < mrows:
            outer = jnp.where(
                line == 0, ch[corner_slot(0, 1), 8 + r:9 + r, :],
                jnp.where(line == mcols - 1, ch[corner_slot(0, -1), 8 + r:9 + r, :], 0.0),
            )
        inner[r] = jnp.concatenate([soft, outer], 1) * laplace(wide, r)
    for r in range(mrows):
        prior[r * probes:(r + 1) * probes, :] = (
            laplace(inner, r) + 0.1 * wide[r]
        )[:, :mcols]

    for s in sides:
        arrive(near_l[s], functools.partial(m_copy, 1 - s))
        arrive(near_l[s], functools.partial(z_copy, 1 - s))

    @pl.when(il != 0)
    def _():
        plane(0, False)

    for z in range(1, depth):
        plane(z, False)

    for b in range(ny):
        at_home = jnp.logical_and(il == 0, iy == b)

        @pl.when(at_home)
        def _():
            prior[...] += part[me]

        @pl.when(jnp.logical_not(at_home))
        def _(b=b):
            remote(
                part.at[0], got.at[b], part_send.at[0], part_recv.at[b], place(ix, me)
            ).wait_recv()
            prior[...] += got[b]

    for r in range(mrows):
        hess[pl.ds(r, probes, stride=mrows), :] = prior[r * probes:(r + 1) * probes, :]

    def sent(near, copy):
        @pl.when(near)
        def _():
            copy().wait_send()

    for s in sides:
        for near, copy in (
            (near_x[s], x_copy), (near_y[s], y_copy), (near_l[s], m_copy),
            (near_l[s], z_copy), (near_x[s], r_copy),
        ):
            sent(near, functools.partial(copy, s))
    for dx, do in corners:
        sent(has(dx, do), functools.partial(c_copy, dx, do))
    for owner in range(no):
        sent(jnp.logical_and(il == 0, me != owner), functools.partial(part_copy, owner))


def shards(velocity, viscosity, friction, owner, cell, directions, stiffness):
    probes = velocity.shape[0]
    depth, rows, cols = viscosity.shape
    mrows, mcols = stiffness.shape
    counts = tuple(lax.axis_size(axis) for axis in ("mapx", "mapy", "layer"))
    no = counts[1] * counts[2]
    nq = probes * 2
    nv = nq * depth
    chunk = min(8, no)
    vmem = pl.BlockSpec(memory_space=pltpu.VMEM)
    image, hessian = pl.pallas_call(
        functools.partial(kernel, counts),
        out_shape=(
            jax.ShapeDtypeStruct((nq, depth, rows, cols), F32),
            jax.ShapeDtypeStruct((probes * mrows, mcols), F32),
        ),
        in_specs=[vmem] * 7,
        out_specs=(vmem, vmem),
        scratch_shapes=[
            pltpu.VMEM((2, nv + 8, cols), F32),
            pltpu.VMEM((2, nv + 8, cols), F32),
            pltpu.VMEM((2, rows, cols), F32),
            pltpu.VMEM((2, rows, cols), F32),
            pltpu.VMEM((2, nq, rows, cols), F32),
            pltpu.VMEM((2, rows, cols), F32),
            pltpu.VMEM((2, 16, mcols), F32),
            pltpu.VMEM((6, 16, mcols), F32),
            pltpu.VMEM((2, 2 * probes + 8, mcols), F32),
            pltpu.VMEM((2, 2 * probes + 8, mcols), F32),
            pltpu.VMEM((rows * probes, cols), F32),
            pltpu.VMEM((2 * mcols, rows * cols), BF16),
            pltpu.VMEM((chunk * (mrows // 2) * 2 * probes, rows * cols), BF16),
            pltpu.VMEM((no, mrows * probes, mcols), F32),
            pltpu.VMEM((counts[1], mrows * probes, mcols), F32),
            pltpu.VMEM((mrows * probes, mcols), F32),
            pltpu.SemaphoreType.DMA((16,)),
            pltpu.SemaphoreType.DMA((16,)),
            pltpu.SemaphoreType.DMA((no,)),
            pltpu.SemaphoreType.DMA((counts[1],)),
        ],
        compiler_params=pltpu.CompilerParams(
            collective_id=0, has_side_effects=True, vmem_limit_bytes=32 << 20
        ),
        name="hessian_action",
    )(
        velocity.reshape(nq, depth, rows, cols),
        viscosity,
        friction,
        owner.reshape(rows, cols),
        cell.reshape(rows, cols),
        directions.reshape(probes * mrows, mcols),
        stiffness,
    )
    return image.reshape(velocity.shape), hessian.reshape(directions.shape)


def solution(mesh):
    return jax.shard_map(
        shards,
        mesh=mesh,
        in_specs=(
            P(None, None, "layer", "mapx", "mapy"),
            P("layer", "mapx", "mapy"),
            P("mapx", "mapy"),
            P("mapx", "mapy", None, None),
            P("mapx", "mapy", None),
            P(None, "mapx", ("mapy", "layer")),
            P("mapx", ("mapy", "layer")),
        ),
        out_specs=(P(None, None, "layer", "mapx", "mapy"), P(None, "mapx", ("mapy", "layer"))),
        check_vma=False,
    )
```

```python
import functools

import jax
import jax.numpy as jnp
from jax import lax
from jax.experimental import pallas as pl
from jax.experimental.pallas import tpu as pltpu
from jax.sharding import PartitionSpec as P

F32 = jnp.float32
BF16 = jnp.bfloat16
X, Y, ZV, ZM, R, C = 0, 2, 4, 6, 8, 10


def corner_slot(dx, do):
    return (dx + 1) * 2 + (0 if do < 0 else 1)


def kernel(
    counts, *refs,
):
    inputs, (img_out, hess_out), staged, (img, hess) = refs[:7], refs[7:9], refs[9:16], refs[16:18]
    (
        xs, xh, ys, yh, zh, mh, cs, ch, rs, rh, tr, onehot, lhs, part, got, prior,
        load, store, send, recv, part_send, part_recv, trace_send, trace_recv,
    ) = refs[18:]
    loads = [
        pltpu.make_async_copy(src, dst, load.at[i])
        for i, (src, dst) in enumerate(zip(inputs, staged))
    ]
    for copy in loads:
        copy.start()
    vel, visc, fric, own, cell, dirs, stiff = staged
    nx, ny, nl = counts
    no = ny * nl
    nq, depth, rows, cols = vel.shape
    nv = nq * depth
    probes = nq // 2
    mrows, mcols = stiff.shape
    halves = probes // 8
    ix, iy, il = lax.axis_index("mapx"), lax.axis_index("mapy"), lax.axis_index("layer")
    me = iy * nl + il

    def place(at_x, owner):
        return (at_x, lax.div(owner, nl), lax.rem(owner, nl))

    low_x, high_x = ix > 0, ix < nx - 1
    low_y, high_y = iy > 0, iy < ny - 1
    low_l, high_l = il > 0, il < nl - 1
    low_o, high_o = me > 0, me < no - 1

    def has(dx, do):
        good_x = {-1: low_x, 1: high_x}.get(dx)
        good_o = {-1: low_o, 1: high_o}.get(do)
        if good_x is None:
            return good_o
        return good_x if good_o is None else jnp.logical_and(good_x, good_o)

    barrier = pltpu.get_barrier_semaphore()
    for step in range(1, no):
        other = lax.rem(me + step, no)
        pl.semaphore_signal(
            barrier, inc=1, device_id=place(ix, other), device_id_type=pl.DeviceIdType.MESH
        )
    greeted = no - 1
    for dx in (-1, 1):
        for do in (-1, 0, 1):
            near = has(dx, do)
            greeted = greeted + near.astype(jnp.int32)

            @pl.when(near)
            def _(dx=dx, do=do):
                pl.semaphore_signal(
                    barrier, inc=1, device_id=place(ix + dx, me + do),
                    device_id_type=pl.DeviceIdType.MESH,
                )

    def remote(src, dst, out_sem, in_sem, device):
        return pltpu.make_async_remote_copy(
            src_ref=src, dst_ref=dst, send_sem=out_sem, recv_sem=in_sem,
            device_id=device, device_id_type=pl.DeviceIdType.MESH,
        )

    def pair(kind, src, dst, side, device):
        return remote(src, dst, send.at[kind + side], recv.at[kind + 1 - side], device)

    def x_copy(side):
        return pair(X, xs.at[side], xh.at[1 - side], side, place(ix + 2 * side - 1, me))

    def r_copy(side):
        return pair(R, rs.at[side], rh.at[1 - side], side, place(ix + 2 * side - 1, me))

    def y_copy(side):
        return pair(Y, ys.at[side], yh.at[1 - side], side, (ix, iy + 2 * side - 1, il))

    def z_copy(side):
        z = 0 if side == 0 else depth - 1
        return pair(ZV, vel.at[:, z], zh.at[1 - side], side, (ix, iy, il + 2 * side - 1))

    def m_copy(side):
        z = 0 if side == 0 else depth - 1
        return pair(ZM, visc.at[z], mh.at[1 - side], side, (ix, iy, il + 2 * side - 1))

    def c_copy(dx, do):
        return remote(
            cs.at[0 if do < 0 else 1], ch.at[corner_slot(-dx, -do)],
            send.at[C + corner_slot(dx, do)], recv.at[C + corner_slot(-dx, -do)],
            place(ix + dx, me + do),
        )

    lane = lax.broadcasted_iota(jnp.int32, (rows, cols), 1)
    sub = lax.broadcasted_iota(jnp.int32, (rows, cols), 0)
    zeros = jnp.zeros((rows, cols), F32)

    loads[0].wait()
    loads[1].wait()
    for z in range(depth):
        xs[0, z * nq:(z + 1) * nq, :] = vel[:, z, 0, :]
        xs[1, z * nq:(z + 1) * nq, :] = vel[:, z, rows - 1, :]
    for side, row in ((0, 0), (1, rows - 1)):
        xs[side, nv:nv + 8, :] = jnp.concatenate(
            [visc[z, row:row + 1, :] for z in range(depth)]
            + [jnp.zeros((8 - depth, cols), F32)], 0,
        )

    def put(value, at, packed):
        here = lane == at
        return (
            jnp.where(here, pltpu.roll(value, at, 1), packed[0]),
            jnp.where(here, pltpu.roll(value, at + 1, 1), packed[1]),
        )

    def pack_y(q, packed):
        for z in range(depth):
            packed = put(vel[q, z], z * nq + q, packed)
        return packed

    packed = lax.fori_loop(0, nq, pack_y, (zeros, zeros), unroll=8)
    for z in range(depth):
        packed = put(visc[z], nv + z, packed)
    ys[0], ys[1] = packed

    loads[5].wait()
    loads[6].wait()
    block = [dirs[pl.ds(r, probes, stride=mrows), :] for r in range(mrows)]
    rim = jnp.concatenate([stiff[...], jnp.zeros((8 - mrows, mcols), F32)], 0)
    for side, first in ((0, 0), (1, mrows - 2)):
        for r in range(2):
            rs[side, r * probes:(r + 1) * probes, :] = block[first + r]
        rs[side, 2 * probes:2 * probes + 8, :] = rim
        cs[side, 8:16, :] = rim
    two = lax.div(lane, 2)
    packed = (zeros, zeros)
    for k in range(mrows * halves):
        value = block[k // halves][(k % halves) * 8:(k % halves) * 8 + 8]
        packed = (
            jnp.where(two == k, pltpu.roll(value, 2 * k, 1) if k else value, packed[0]),
            jnp.where(two == k, pltpu.roll(value, 2 * k + 2, 1), packed[1]),
        )
    cs[0, 0:8, :], cs[1, 0:8, :] = packed

    pl.semaphore_wait(barrier, greeted)

    def when_near(near, copy):
        @pl.when(near)
        def _():
            copy().start()

    sides = (0, 1)
    near_x, near_y, near_l = (low_x, high_x), (low_y, high_y), (low_l, high_l)
    corners = [(dx, do) for dx in (-1, 0, 1) for do in (-1, 1)]
    for s in sides:
        when_near(near_x[s], functools.partial(x_copy, s))
        when_near(near_y[s], functools.partial(y_copy, s))
    for s in sides:
        when_near(near_l[s], functools.partial(m_copy, s))
        when_near(near_l[s], functools.partial(z_copy, s))
    for s in sides:
        when_near(near_x[s], functools.partial(r_copy, s))
    for dx, do in corners:
        when_near(has(dx, do), functools.partial(c_copy, dx, do))

    def zero_unless(near, ref, at):
        @pl.when(jnp.logical_not(near))
        def _():
            ref[at] = jnp.zeros(ref.shape[1:], F32)

    for s in sides:
        zero_unless(near_x[s], xh, s)
        zero_unless(near_y[s], yh, s)
        zero_unless(near_l[s], zh, s)
        zero_unless(near_l[s], mh, s)
        zero_unless(near_x[s], rh, s)
    for dx, do in corners:
        zero_unless(has(dx, do), ch, corner_slot(dx, do))

    span = 2 * mcols
    pairs = mrows // 2
    for i in (2, 3, 4):
        loads[i].wait()
    cells = cell[...]
    low = lax.rem(cells, span)
    owners = own[...]
    group = jnp.where(
        lax.rem(owners, nl) == il, lax.div(owners, nl) * pairs + lax.div(cells, span), -1
    )
    number = lax.broadcasted_iota(jnp.int32, (span, cols), 0)
    for x in range(rows):
        onehot[:, x * cols:(x + 1) * cols] = jnp.where(
            number == low[x:x + 1, :], 1.0, 0.0
        ).astype(BF16)

    def arrive(near, copy):
        @pl.when(near)
        def _():
            copy().wait_recv()

    def beside(value, index, halo_rows, halo_lanes):
        down = jnp.where(sub == 0, halo_rows[0], pltpu.roll(value, 1, 0))
        up = jnp.where(sub == rows - 1, halo_rows[1], pltpu.roll(value, rows - 1, 0))
        left = jnp.where(
            lane == 0, pltpu.roll(halo_lanes[0], cols - index, 1), pltpu.roll(value, 1, 1)
        )
        right = jnp.where(
            lane == cols - 1,
            pltpu.roll(halo_lanes[1], cols - 1 - index, 1),
            pltpu.roll(value, cols - 1, 1),
        )
        return down, up, left, right

    def rows_at(index):
        return tuple(
            jnp.broadcast_to(xh[s, pl.ds(index, 1), :], (rows, cols)) for s in sides
        )

    def image_copy(z):
        return pltpu.make_async_copy(img.at[:, z], img_out.at[:, z], store.at[z])

    def plane(z, trace):
        lanes = (yh[0], yh[1])
        here = visc[z]
        around = beside(here, nv + z, rows_at(nv + z), lanes)
        mean = [0.5 * (here + other) for other in around]
        down_z = here + (mh[0] if z == 0 else visc[z - 1])
        up_z = here + (mh[1] if z == depth - 1 else visc[z + 1])
        weights = (
            (mean[0], mean[1], 0.25 * mean[2], 0.25 * mean[3]),
            (0.25 * mean[0], 0.25 * mean[1], mean[2], mean[3]),
        )
        rub = fric[...]

        def probe(p, carry):
            both = None
            for c in range(2):
                q = p * 2 + c
                value = vel[q, z]
                below = zh[0, q] if z == 0 else vel[q, z - 1]
                above = zh[1, q] if z == depth - 1 else vel[q, z + 1]
                index = z * nq + q
                total = up_z * (value - above) + down_z * (value - below)
                for weight, other in zip(
                    weights[c], beside(value, index, rows_at(index), lanes)
                ):
                    total = total + weight * (value - other)
                img[q, z] = total
                both = total if both is None else both + total
            if trace:
                tr[pl.ds(p, rows, stride=probes), :] = rub * both
            return carry

        lax.fori_loop(0, probes, probe, 0, unroll=4)
        image_copy(z).start()

    for s in sides:
        arrive(near_x[s], functools.partial(x_copy, 1 - s))
        arrive(near_y[s], functools.partial(y_copy, 1 - s))

    def smooth():
        for s in sides:
            arrive(near_x[s], functools.partial(r_copy, 1 - s))
        for dx, do in corners:
            arrive(has(dx, do), functools.partial(c_copy, -dx, -do))

        def edge(dx, r):
            left, right = ch[corner_slot(dx, -1), 0:8, :], ch[corner_slot(dx, 1), 0:8, :]
            halfs = []
            for h in range(halves):
                k = 2 * (r * halves + h)
                from_right = pltpu.roll(right, mcols - k, 1) if k else right
                from_left = pltpu.roll(left, mcols - 2 - k, 1)
                halfs.append(
                    jnp.where(lane < 2, from_right, jnp.where(lane >= mcols - 2, from_left, 0.0))
                )
            return jnp.concatenate(halfs, 0)

        wide = {}
        for r in range(2):
            wide[r - 2] = jnp.concatenate(
                [rh[0, r * probes:(r + 1) * probes, :], edge(-1, mrows - 2 + r)], 1
            )
            wide[mrows + r] = jnp.concatenate(
                [rh[1, r * probes:(r + 1) * probes, :], edge(1, r)], 1
            )
        for r in range(mrows):
            wide[r] = jnp.concatenate([dirs[pl.ds(r, probes, stride=mrows), :], edge(0, r)], 1)

        def laplace(field, r):
            return (
                4.0 * field[r] - field[r - 1] - field[r + 1]
                - pltpu.roll(field[r], 1, 1) - pltpu.roll(field[r], 2 * mcols - 1, 1)
            )

        line = lax.broadcasted_iota(jnp.int32, (1, mcols), 1)
        inner = {}
        for r in range(-1, mrows + 1):
            if r < 0:
                soft = rh[0, 2 * probes + mrows - 1:2 * probes + mrows, :]
            elif r == mrows:
                soft = rh[1, 2 * probes:2 * probes + 1, :]
            else:
                soft = stiff[r:r + 1, :]
            outer = jnp.zeros((1, mcols), F32)
            if 0 <= r < mrows:
                outer = jnp.where(
                    line == 0, ch[corner_slot(0, 1), 8 + r:9 + r, :],
                    jnp.where(line == mcols - 1, ch[corner_slot(0, -1), 8 + r:9 + r, :], 0.0),
                )
            inner[r] = jnp.concatenate([soft, outer], 1) * laplace(wide, r)
        for r in range(mrows):
            prior[r * probes:(r + 1) * probes, :] = (
                laplace(inner, r) + 0.1 * wide[r]
            )[:, :mcols]

    chunk = min(8, ny)
    tall = 2 * probes

    def trace_copy(layer):
        return remote(
            tr, tr, trace_send.at[layer], trace_recv, (ix, iy, layer)
        )

    def part_copy(to):
        return remote(
            part.at[to], got.at[iy], part_send.at[to], part_recv.at[iy], (ix, to, il)
        )

    @pl.when(il == 0)
    def _():
        plane(0, True)
        for layer in range(1, nl):
            trace_copy(layer).start()

    @pl.when(il != 0)
    def _():
        smooth()
        trace_copy(0).wait_recv()

    coarse, fine = [], []
    for x in range(rows):
        values = tr[x * probes:(x + 1) * probes, :]
        coarse.append(values.astype(BF16).astype(F32))
        fine.append(values - coarse[-1])

    def reduce_chunk(base):
        for g in range(chunk * pairs):
            for x in range(rows):
                mine = group[x:x + 1, :] == base * pairs + g
                lhs[g * tall:(g + 1) * tall, x * cols:(x + 1) * cols] = jnp.concatenate(
                    [jnp.where(mine, coarse[x], 0.0), jnp.where(mine, fine[x], 0.0)], 0
                ).astype(BF16)
        sums = lax.dot_general(
            lhs[...], onehot[...], (((1,), (1,)), ((), ())), preferred_element_type=F32
        )
        for j in range(chunk):
            for h in range(pairs):
                at = (j * pairs + h) * tall
                both = sums[at:at + probes] + sums[at + probes:at + tall]
                for k in range(2):
                    row = (2 * h + k) * probes
                    part[base + j, row:row + probes, :] = both[:, k * mcols:(k + 1) * mcols]

    if ny == chunk:
        reduce_chunk(0)
    else:
        def chunk_step(i, carry):
            reduce_chunk(i * chunk)
            return carry

        lax.fori_loop(0, ny // chunk, chunk_step, 0)
    steps = sorted(range(1, ny), key=lambda step: abs(step - ny // 2))
    for step in steps:
        part_copy(lax.rem(iy + step, ny)).start()

    @pl.when(il == 0)
    def _():
        smooth()

    for s in sides:
        arrive(near_l[s], functools.partial(m_copy, 1 - s))
        arrive(near_l[s], functools.partial(z_copy, 1 - s))

    @pl.when(il != 0)
    def _():
        plane(0, False)

    for z in range(1, depth):
        plane(z, False)

    for step in reversed(steps):
        b = lax.rem(iy + step, ny)
        remote(
            part.at[0], got.at[b], part_send.at[0], part_recv.at[b], (ix, b, il)
        ).wait_recv()
    for r in range(mrows):
        at = slice(r * probes, (r + 1) * probes)
        total = prior[at, :] + part[iy, at, :]
        for step in range(1, ny):
            total = total + got[lax.rem(iy + step, ny), at, :]
        hess[pl.ds(r, probes, stride=mrows), :] = total
    hess_copy = pltpu.make_async_copy(hess, hess_out, store.at[depth])
    hess_copy.start()

    def sent(near, copy):
        @pl.when(near)
        def _():
            copy().wait_send()

    for s in sides:
        for near, copy in (
            (near_x[s], x_copy), (near_y[s], y_copy), (near_l[s], m_copy),
            (near_l[s], z_copy), (near_x[s], r_copy),
        ):
            sent(near, functools.partial(copy, s))
    for dx, do in corners:
        sent(has(dx, do), functools.partial(c_copy, dx, do))
    for step in steps:
        part_copy(lax.rem(iy + step, ny)).wait_send()
    for layer in range(1, nl):
        sent(il == 0, functools.partial(trace_copy, layer))
    for z in range(depth):
        image_copy(z).wait()
    hess_copy.wait()


def deliver_kernel(image, hessian, image_out, hessian_out, sems):
    quarter = image.shape[0] // 4
    copies = [pltpu.make_async_copy(hessian, hessian_out, sems.at[4])]
    for i in range(4):
        rows = pl.ds(i * quarter, quarter)
        copies.append(pltpu.make_async_copy(image.at[rows], image_out.at[rows], sems.at[i]))
    for copy in copies:
        copy.start()
    for copy in copies:
        copy.wait()


def deliver(image, hessian):
    whole = pl.BlockSpec(memory_space=pltpu.HBM)
    return pl.pallas_call(
        deliver_kernel,
        out_shape=tuple(jax.ShapeDtypeStruct(a.shape, a.dtype) for a in (image, hessian)),
        in_specs=[whole, whole],
        out_specs=(whole, whole),
        scratch_shapes=[pltpu.SemaphoreType.DMA((5,))],
        compiler_params=pltpu.CompilerParams(vmem_limit_bytes=60 << 20),
        name="deliver",
    )(image, hessian)


def shards(velocity, viscosity, friction, owner, cell, directions, stiffness):
    probes = velocity.shape[0]
    depth, rows, cols = viscosity.shape
    mrows, mcols = stiffness.shape
    counts = tuple(lax.axis_size(axis) for axis in ("mapx", "mapy", "layer"))
    nq = probes * 2
    nv = nq * depth
    chunk = min(8, counts[1])
    whole = pl.BlockSpec(memory_space=pltpu.HBM)
    image, hessian = pl.pallas_call(
        functools.partial(kernel, counts),
        out_shape=(
            jax.ShapeDtypeStruct((nq, depth, rows, cols), F32),
            jax.ShapeDtypeStruct((probes * mrows, mcols), F32),
        ),
        in_specs=[whole] * 7,
        out_specs=(whole, whole),
        scratch_shapes=[
            pltpu.VMEM((nq, depth, rows, cols), F32),
            pltpu.VMEM((depth, rows, cols), F32),
            pltpu.VMEM((rows, cols), F32),
            pltpu.VMEM((rows, cols), jnp.int32),
            pltpu.VMEM((rows, cols), jnp.int32),
            pltpu.VMEM((probes * mrows, mcols), F32),
            pltpu.VMEM((mrows, mcols), F32),
            pltpu.VMEM((nq, depth, rows, cols), F32),
            pltpu.VMEM((probes * mrows, mcols), F32),
            pltpu.VMEM((2, nv + 8, cols), F32),
            pltpu.VMEM((2, nv + 8, cols), F32),
            pltpu.VMEM((2, rows, cols), F32),
            pltpu.VMEM((2, rows, cols), F32),
            pltpu.VMEM((2, nq, rows, cols), F32),
            pltpu.VMEM((2, rows, cols), F32),
            pltpu.VMEM((2, 16, mcols), F32),
            pltpu.VMEM((6, 16, mcols), F32),
            pltpu.VMEM((2, 2 * probes + 8, mcols), F32),
            pltpu.VMEM((2, 2 * probes + 8, mcols), F32),
            pltpu.VMEM((rows * probes, cols), F32),
            pltpu.VMEM((2 * mcols, rows * cols), BF16),
            pltpu.VMEM((chunk * (mrows // 2) * 2 * probes, rows * cols), BF16),
            pltpu.VMEM((counts[1], mrows * probes, mcols), F32),
            pltpu.VMEM((counts[1], mrows * probes, mcols), F32),
            pltpu.VMEM((mrows * probes, mcols), F32),
            pltpu.SemaphoreType.DMA((7,)),
            pltpu.SemaphoreType.DMA((depth + 1,)),
            pltpu.SemaphoreType.DMA((16,)),
            pltpu.SemaphoreType.DMA((16,)),
            pltpu.SemaphoreType.DMA((counts[1],)),
            pltpu.SemaphoreType.DMA((counts[1],)),
            pltpu.SemaphoreType.DMA((counts[2],)),
            pltpu.SemaphoreType.DMA,
        ],
        compiler_params=pltpu.CompilerParams(
            collective_id=0, has_side_effects=True, vmem_limit_bytes=60 << 20
        ),
        name="hessian_action",
    )(
        velocity.reshape(nq, depth, rows, cols),
        viscosity,
        friction,
        owner.reshape(rows, cols),
        cell.reshape(rows, cols),
        directions.reshape(probes * mrows, mcols),
        stiffness,
    )
    image, hessian = deliver(image, hessian)
    return image.reshape(velocity.shape), hessian.reshape(directions.shape)


def solution(mesh):
    return jax.shard_map(
        shards,
        mesh=mesh,
        in_specs=(
            P(None, None, "layer", "mapx", "mapy"),
            P("layer", "mapx", "mapy"),
            P("mapx", "mapy"),
            P("mapx", "mapy", None, None),
            P("mapx", "mapy", None),
            P(None, "mapx", ("mapy", "layer")),
            P("mapx", ("mapy", "layer")),
        ),
        out_specs=(P(None, None, "layer", "mapx", "mapy"), P(None, "mapx", ("mapy", "layer"))),
        check_vma=False,
    )
```

```python
import functools

import jax
import jax.numpy as jnp
from jax import lax
from jax.experimental import pallas as pl
from jax.experimental.pallas import tpu as pltpu
from jax.sharding import PartitionSpec as P

F32 = jnp.float32
BF16 = jnp.bfloat16
X, Y, ZV, ZM, R, C = 0, 2, 4, 6, 8, 10


def corner_slot(dx, do):
    return (dx + 1) * 2 + (0 if do < 0 else 1)


def kernel(
    counts, *refs,
):
    inputs, (img_out, hess_out), staged, (img, hess) = refs[:7], refs[7:9], refs[9:16], refs[16:18]
    (
        xs, xh, ys, yh, zh, mh, cs, ch, rs, rh, tr, onehot, lhs, part, got, prior,
        load, store, send, recv, part_send, part_recv, trace_send, trace_recv,
    ) = refs[18:]
    loads = [
        pltpu.make_async_copy(src, dst, load.at[i])
        for i, (src, dst) in enumerate(zip(inputs, staged))
    ]
    for copy in loads:
        copy.start()
    vel, visc, fric, own, cell, dirs, stiff = staged
    nx, ny, nl = counts
    no = ny * nl
    nq, depth, rows, cols = vel.shape
    nv = nq * depth
    probes = nq // 2
    mrows, mcols = stiff.shape
    halves = probes // 8
    ix, iy, il = lax.axis_index("mapx"), lax.axis_index("mapy"), lax.axis_index("layer")
    me = iy * nl + il

    def place(at_x, owner):
        return (at_x, lax.div(owner, nl), lax.rem(owner, nl))

    low_x, high_x = ix > 0, ix < nx - 1
    low_y, high_y = iy > 0, iy < ny - 1
    low_l, high_l = il > 0, il < nl - 1
    low_o, high_o = me > 0, me < no - 1

    def has(dx, do):
        good_x = {-1: low_x, 1: high_x}.get(dx)
        good_o = {-1: low_o, 1: high_o}.get(do)
        if good_x is None:
            return good_o
        return good_x if good_o is None else jnp.logical_and(good_x, good_o)

    barrier = pltpu.get_barrier_semaphore()
    for step in range(1, ny):
        pl.semaphore_signal(barrier, inc=1, device_id=(ix, lax.rem(iy + step, ny), il), device_id_type=pl.DeviceIdType.MESH)
    for step in range(1, nl):
        pl.semaphore_signal(barrier, inc=1, device_id=(ix, iy, lax.rem(il + step, nl)), device_id_type=pl.DeviceIdType.MESH)
    greeted = ny - 1 + nl - 1
    for dx in (-1, 0, 1):
        for do in ((-1, 1) if dx == 0 else (-1, 0, 1)):
            near = has(dx, do)
            greeted = greeted + near.astype(jnp.int32)

            @pl.when(near)
            def _(dx=dx, do=do):
                pl.semaphore_signal(
                    barrier, inc=1, device_id=place(ix + dx, me + do),
                    device_id_type=pl.DeviceIdType.MESH,
                )

    def remote(src, dst, out_sem, in_sem, device):
        return pltpu.make_async_remote_copy(
            src_ref=src, dst_ref=dst, send_sem=out_sem, recv_sem=in_sem,
            device_id=device, device_id_type=pl.DeviceIdType.MESH,
        )

    def pair(kind, src, dst, side, device):
        return remote(src, dst, send.at[kind + side], recv.at[kind + 1 - side], device)

    def x_copy(side):
        return pair(X, xs.at[side], xh.at[1 - side], side, place(ix + 2 * side - 1, me))

    def r_copy(side):
        return pair(R, rs.at[side], rh.at[1 - side], side, place(ix + 2 * side - 1, me))

    def y_copy(side):
        return pair(Y, ys.at[side], yh.at[1 - side], side, (ix, iy + 2 * side - 1, il))

    def z_copy(side):
        z = 0 if side == 0 else depth - 1
        return pair(ZV, vel.at[:, z], zh.at[1 - side], side, (ix, iy, il + 2 * side - 1))

    def m_copy(side):
        z = 0 if side == 0 else depth - 1
        return pair(ZM, visc.at[z], mh.at[1 - side], side, (ix, iy, il + 2 * side - 1))

    def c_copy(dx, do):
        return remote(
            cs.at[0 if do < 0 else 1], ch.at[corner_slot(-dx, -do)],
            send.at[C + corner_slot(dx, do)], recv.at[C + corner_slot(-dx, -do)],
            place(ix + dx, me + do),
        )

    lane = lax.broadcasted_iota(jnp.int32, (rows, cols), 1)
    sub = lax.broadcasted_iota(jnp.int32, (rows, cols), 0)
    zeros = jnp.zeros((rows, cols), F32)

    loads[0].wait()
    loads[1].wait()
    for z in range(depth):
        xs[0, z * nq:(z + 1) * nq, :] = vel[:, z, 0, :]
        xs[1, z * nq:(z + 1) * nq, :] = vel[:, z, rows - 1, :]
    for side, row in ((0, 0), (1, rows - 1)):
        xs[side, nv:nv + 8, :] = jnp.concatenate(
            [visc[z, row:row + 1, :] for z in range(depth)]
            + [jnp.zeros((8 - depth, cols), F32)], 0,
        )

    def put(value, at, packed):
        here = lane == at
        return (
            jnp.where(here, pltpu.roll(value, at, 1), packed[0]),
            jnp.where(here, pltpu.roll(value, at + 1, 1), packed[1]),
        )

    def pack_y(q, packed):
        for z in range(depth):
            packed = put(vel[q, z], z * nq + q, packed)
        return packed

    packed = lax.fori_loop(0, nq, pack_y, (zeros, zeros), unroll=8)
    for z in range(depth):
        packed = put(visc[z], nv + z, packed)
    ys[0], ys[1] = packed

    loads[5].wait()
    loads[6].wait()
    block = [dirs[pl.ds(r, probes, stride=mrows), :] for r in range(mrows)]
    rim = jnp.concatenate([stiff[...], jnp.zeros((8 - mrows, mcols), F32)], 0)
    for side, first in ((0, 0), (1, mrows - 2)):
        for r in range(2):
            rs[side, r * probes:(r + 1) * probes, :] = block[first + r]
        rs[side, 2 * probes:2 * probes + 8, :] = rim
        cs[side, 8:16, :] = rim
    two = lax.div(lane, 2)
    packed = (zeros, zeros)
    for k in range(mrows * halves):
        value = block[k // halves][(k % halves) * 8:(k % halves) * 8 + 8]
        packed = (
            jnp.where(two == k, pltpu.roll(value, 2 * k, 1) if k else value, packed[0]),
            jnp.where(two == k, pltpu.roll(value, 2 * k + 2, 1), packed[1]),
        )
    cs[0, 0:8, :], cs[1, 0:8, :] = packed

    pl.semaphore_wait(barrier, greeted)

    def when_near(near, copy):
        @pl.when(near)
        def _():
            copy().start()

    sides = (0, 1)
    near_x, near_y, near_l = (low_x, high_x), (low_y, high_y), (low_l, high_l)
    corners = [(dx, do) for dx in (-1, 0, 1) for do in (-1, 1)]
    for s in sides:
        when_near(near_x[s], functools.partial(x_copy, s))
        when_near(near_y[s], functools.partial(y_copy, s))
    for s in sides:
        when_near(near_l[s], functools.partial(m_copy, s))
        when_near(near_l[s], functools.partial(z_copy, s))
    for s in sides:
        when_near(near_x[s], functools.partial(r_copy, s))
    for dx, do in corners:
        when_near(has(dx, do), functools.partial(c_copy, dx, do))

    def zero_unless(near, ref, at):
        @pl.when(jnp.logical_not(near))
        def _():
            ref[at] = jnp.zeros(ref.shape[1:], F32)

    for s in sides:
        zero_unless(near_x[s], xh, s)
        zero_unless(near_y[s], yh, s)
        zero_unless(near_l[s], zh, s)
        zero_unless(near_l[s], mh, s)
        zero_unless(near_x[s], rh, s)
    for dx, do in corners:
        zero_unless(has(dx, do), ch, corner_slot(dx, do))

    span = 2 * mcols
    pairs = mrows // 2
    for i in (2, 3, 4):
        loads[i].wait()
    cells = cell[...]
    low = lax.rem(cells, span)
    owners = own[...]
    group = jnp.where(
        lax.rem(owners, nl) == il, lax.div(owners, nl) * pairs + lax.div(cells, span), -1
    )
    number = lax.broadcasted_iota(jnp.int32, (span, cols), 0)
    for x in range(rows):
        onehot[:, x * cols:(x + 1) * cols] = jnp.where(
            number == low[x:x + 1, :], 1.0, 0.0
        ).astype(BF16)

    def arrive(near, copy):
        @pl.when(near)
        def _():
            copy().wait_recv()

    def beside(value, index, halo_rows, halo_lanes):
        down = jnp.where(sub == 0, halo_rows[0], pltpu.roll(value, 1, 0))
        up = jnp.where(sub == rows - 1, halo_rows[1], pltpu.roll(value, rows - 1, 0))
        left = jnp.where(
            lane == 0, pltpu.roll(halo_lanes[0], cols - index, 1), pltpu.roll(value, 1, 1)
        )
        right = jnp.where(
            lane == cols - 1,
            pltpu.roll(halo_lanes[1], cols - 1 - index, 1),
            pltpu.roll(value, cols - 1, 1),
        )
        return down, up, left, right

    def rows_at(index):
        return tuple(
            jnp.broadcast_to(xh[s, pl.ds(index, 1), :], (rows, cols)) for s in sides
        )

    def image_copy(z):
        return pltpu.make_async_copy(img.at[:, z], img_out.at[:, z], store.at[z])

    def plane(z, trace):
        lanes = (yh[0], yh[1])
        here = visc[z]
        around = beside(here, nv + z, rows_at(nv + z), lanes)
        mean = [0.5 * (here + other) for other in around]
        down_z = here + (mh[0] if z == 0 else visc[z - 1])
        up_z = here + (mh[1] if z == depth - 1 else visc[z + 1])
        weights = (
            (mean[0], mean[1], 0.25 * mean[2], 0.25 * mean[3]),
            (0.25 * mean[0], 0.25 * mean[1], mean[2], mean[3]),
        )
        rub = fric[...]

        def probe(p, carry):
            both = None
            for c in range(2):
                q = p * 2 + c
                value = vel[q, z]
                below = zh[0, q] if z == 0 else vel[q, z - 1]
                above = zh[1, q] if z == depth - 1 else vel[q, z + 1]
                index = z * nq + q
                total = up_z * (value - above) + down_z * (value - below)
                for weight, other in zip(
                    weights[c], beside(value, index, rows_at(index), lanes)
                ):
                    total = total + weight * (value - other)
                img[q, z] = total
                both = total if both is None else both + total
            if trace:
                tr[pl.ds(p, rows, stride=probes), :] = rub * both
            return carry

        lax.fori_loop(0, probes, probe, 0, unroll=4)
        image_copy(z).start()

    for s in sides:
        arrive(near_x[s], functools.partial(x_copy, 1 - s))
        arrive(near_y[s], functools.partial(y_copy, 1 - s))

    def smooth():
        for s in sides:
            arrive(near_x[s], functools.partial(r_copy, 1 - s))
        for dx, do in corners:
            arrive(has(dx, do), functools.partial(c_copy, -dx, -do))

        def edge(dx, r):
            left, right = ch[corner_slot(dx, -1), 0:8, :], ch[corner_slot(dx, 1), 0:8, :]
            halfs = []
            for h in range(halves):
                k = 2 * (r * halves + h)
                from_right = pltpu.roll(right, mcols - k, 1) if k else right
                from_left = pltpu.roll(left, mcols - 2 - k, 1)
                halfs.append(
                    jnp.where(lane < 2, from_right, jnp.where(lane >= mcols - 2, from_left, 0.0))
                )
            return jnp.concatenate(halfs, 0)

        wide = {}
        for r in range(2):
            wide[r - 2] = jnp.concatenate(
                [rh[0, r * probes:(r + 1) * probes, :], edge(-1, mrows - 2 + r)], 1
            )
            wide[mrows + r] = jnp.concatenate(
                [rh[1, r * probes:(r + 1) * probes, :], edge(1, r)], 1
            )
        for r in range(mrows):
            wide[r] = jnp.concatenate([dirs[pl.ds(r, probes, stride=mrows), :], edge(0, r)], 1)

        def laplace(field, r):
            return (
                4.0 * field[r] - field[r - 1] - field[r + 1]
                - pltpu.roll(field[r], 1, 1) - pltpu.roll(field[r], 2 * mcols - 1, 1)
            )

        line = lax.broadcasted_iota(jnp.int32, (1, mcols), 1)
        inner = {}
        for r in range(-1, mrows + 1):
            if r < 0:
                soft = rh[0, 2 * probes + mrows - 1:2 * probes + mrows, :]
            elif r == mrows:
                soft = rh[1, 2 * probes:2 * probes + 1, :]
            else:
                soft = stiff[r:r + 1, :]
            outer = jnp.zeros((1, mcols), F32)
            if 0 <= r < mrows:
                outer = jnp.where(
                    line == 0, ch[corner_slot(0, 1), 8 + r:9 + r, :],
                    jnp.where(line == mcols - 1, ch[corner_slot(0, -1), 8 + r:9 + r, :], 0.0),
                )
            inner[r] = jnp.concatenate([soft, outer], 1) * laplace(wide, r)
        for r in range(mrows):
            prior[r * probes:(r + 1) * probes, :] = (
                laplace(inner, r) + 0.1 * wide[r]
            )[:, :mcols]

    def arrive_layers():
        for s in reversed(sides):
            arrive(near_l[s], functools.partial(m_copy, 1 - s))
            arrive(near_l[s], functools.partial(z_copy, 1 - s))

    chunk = min(8, ny)
    tall = 2 * probes

    def trace_copy(layer):
        return remote(
            tr, tr, trace_send.at[layer], trace_recv, (ix, iy, layer)
        )

    def part_copy(to):
        return remote(
            part.at[to], got.at[iy], part_send.at[to], part_recv.at[iy], (ix, to, il)
        )

    @pl.when(il == 0)
    def _():
        plane(0, True)
        for layer in range(1, nl):
            trace_copy(layer).start()

    @pl.when(il != 0)
    def _():
        smooth()
        arrive_layers()
        for z in reversed(range(depth)):
            plane(z, False)
        trace_copy(0).wait_recv()

    coarse, fine = [], []
    for x in range(rows):
        values = tr[x * probes:(x + 1) * probes, :]
        coarse.append(values.astype(BF16).astype(F32))
        fine.append(values - coarse[-1])

    def reduce_chunk(base):
        for g in range(chunk * pairs):
            for x in range(rows):
                mine = group[x:x + 1, :] == base * pairs + g
                lhs[g * tall:(g + 1) * tall, x * cols:(x + 1) * cols] = jnp.concatenate(
                    [jnp.where(mine, coarse[x], 0.0), jnp.where(mine, fine[x], 0.0)], 0
                ).astype(BF16)
        sums = lax.dot_general(
            lhs[...], onehot[...], (((1,), (1,)), ((), ())), preferred_element_type=F32
        )
        for j in range(chunk):
            for h in range(pairs):
                at = (j * pairs + h) * tall
                both = sums[at:at + probes] + sums[at + probes:at + tall]
                for k in range(2):
                    row = (2 * h + k) * probes
                    part[base + j, row:row + probes, :] = both[:, k * mcols:(k + 1) * mcols]

    if ny == chunk:
        reduce_chunk(0)
    else:
        def chunk_step(i, carry):
            reduce_chunk(i * chunk)
            return carry

        lax.fori_loop(0, ny // chunk, chunk_step, 0)
    steps = sorted(range(1, ny), key=lambda step: abs(step - ny // 2))
    for step in steps:
        part_copy(lax.rem(iy + step, ny)).start()

    @pl.when(il == 0)
    def _():
        smooth()
        arrive_layers()
        for z in range(1, depth):
            plane(z, False)

    for step in reversed(steps):
        b = lax.rem(iy + step, ny)
        remote(
            part.at[0], got.at[b], part_send.at[0], part_recv.at[b], (ix, b, il)
        ).wait_recv()
    for r in range(mrows):
        at = slice(r * probes, (r + 1) * probes)
        total = prior[at, :] + part[iy, at, :]
        for step in range(1, ny):
            total = total + got[lax.rem(iy + step, ny), at, :]
        hess[pl.ds(r, probes, stride=mrows), :] = total
    hess_copy = pltpu.make_async_copy(hess, hess_out, store.at[depth])
    hess_copy.start()

    def sent(near, copy):
        @pl.when(near)
        def _():
            copy().wait_send()

    for s in sides:
        for near, copy in (
            (near_x[s], x_copy), (near_y[s], y_copy), (near_l[s], m_copy),
            (near_l[s], z_copy), (near_x[s], r_copy),
        ):
            sent(near, functools.partial(copy, s))
    for dx, do in corners:
        sent(has(dx, do), functools.partial(c_copy, dx, do))
    for step in steps:
        part_copy(lax.rem(iy + step, ny)).wait_send()
    for layer in range(1, nl):
        sent(il == 0, functools.partial(trace_copy, layer))
    for z in range(depth):
        image_copy(z).wait()
    hess_copy.wait()


def deliver_kernel(image, hessian, image_out, hessian_out, image_in, hessian_in, first, second):
    quarter = image.shape[0] // 4
    steps = [(hessian, hessian_in, hessian_out)]
    for i in range(4):
        rows = pl.ds(i * quarter, quarter)
        steps.append((image.at[rows], image_in.at[rows], image_out.at[rows]))
    loads = [
        pltpu.make_async_copy(src, mid, first.at[i]) for i, (src, mid, _) in enumerate(steps)
    ]
    stores = [
        pltpu.make_async_copy(mid, dst, second.at[i]) for i, (_, mid, dst) in enumerate(steps)
    ]
    for copy in loads:
        copy.start()
    for load, store in zip(loads, stores):
        load.wait()
        store.start()
    for copy in stores:
        copy.wait()


def deliver(image, hessian):
    whole = pl.BlockSpec(memory_space=pltpu.HBM)
    return pl.pallas_call(
        deliver_kernel,
        out_shape=tuple(jax.ShapeDtypeStruct(a.shape, a.dtype) for a in (image, hessian)),
        in_specs=[whole, whole],
        out_specs=(whole, whole),
        scratch_shapes=[
            pltpu.VMEM(image.shape, F32),
            pltpu.VMEM(hessian.shape, F32),
            pltpu.SemaphoreType.DMA((5,)),
            pltpu.SemaphoreType.DMA((5,)),
        ],
        compiler_params=pltpu.CompilerParams(vmem_limit_bytes=60 << 20),
        name="deliver",
    )(image, hessian)


def shards(velocity, viscosity, friction, owner, cell, directions, stiffness):
    probes = velocity.shape[0]
    depth, rows, cols = viscosity.shape
    mrows, mcols = stiffness.shape
    counts = tuple(lax.axis_size(axis) for axis in ("mapx", "mapy", "layer"))
    nq = probes * 2
    nv = nq * depth
    chunk = min(8, counts[1])
    whole = pl.BlockSpec(memory_space=pltpu.HBM)
    image, hessian = pl.pallas_call(
        functools.partial(kernel, counts),
        out_shape=(
            jax.ShapeDtypeStruct((nq, depth, rows, cols), F32),
            jax.ShapeDtypeStruct((probes * mrows, mcols), F32),
        ),
        in_specs=[whole] * 7,
        out_specs=(whole, whole),
        scratch_shapes=[
            pltpu.VMEM((nq, depth, rows, cols), F32),
            pltpu.VMEM((depth, rows, cols), F32),
            pltpu.VMEM((rows, cols), F32),
            pltpu.VMEM((rows, cols), jnp.int32),
            pltpu.VMEM((rows, cols), jnp.int32),
            pltpu.VMEM((probes * mrows, mcols), F32),
            pltpu.VMEM((mrows, mcols), F32),
            pltpu.VMEM((nq, depth, rows, cols), F32),
            pltpu.VMEM((probes * mrows, mcols), F32),
            pltpu.VMEM((2, nv + 8, cols), F32),
            pltpu.VMEM((2, nv + 8, cols), F32),
            pltpu.VMEM((2, rows, cols), F32),
            pltpu.VMEM((2, rows, cols), F32),
            pltpu.VMEM((2, nq, rows, cols), F32),
            pltpu.VMEM((2, rows, cols), F32),
            pltpu.VMEM((2, 16, mcols), F32),
            pltpu.VMEM((6, 16, mcols), F32),
            pltpu.VMEM((2, 2 * probes + 8, mcols), F32),
            pltpu.VMEM((2, 2 * probes + 8, mcols), F32),
            pltpu.VMEM((rows * probes, cols), F32),
            pltpu.VMEM((2 * mcols, rows * cols), BF16),
            pltpu.VMEM((chunk * (mrows // 2) * 2 * probes, rows * cols), BF16),
            pltpu.VMEM((counts[1], mrows * probes, mcols), F32),
            pltpu.VMEM((counts[1], mrows * probes, mcols), F32),
            pltpu.VMEM((mrows * probes, mcols), F32),
            pltpu.SemaphoreType.DMA((7,)),
            pltpu.SemaphoreType.DMA((depth + 1,)),
            pltpu.SemaphoreType.DMA((16,)),
            pltpu.SemaphoreType.DMA((16,)),
            pltpu.SemaphoreType.DMA((counts[1],)),
            pltpu.SemaphoreType.DMA((counts[1],)),
            pltpu.SemaphoreType.DMA((counts[2],)),
            pltpu.SemaphoreType.DMA,
        ],
        compiler_params=pltpu.CompilerParams(
            collective_id=0, has_side_effects=True, vmem_limit_bytes=60 << 20
        ),
        name="hessian_action",
    )(
        velocity.reshape(nq, depth, rows, cols),
        viscosity,
        friction,
        owner.reshape(rows, cols),
        cell.reshape(rows, cols),
        directions.reshape(probes * mrows, mcols),
        stiffness,
    )
    image, hessian = deliver(image, hessian)
    return image.reshape(velocity.shape), hessian.reshape(directions.shape)


def solution(mesh):
    return jax.shard_map(
        shards,
        mesh=mesh,
        in_specs=(
            P(None, None, "layer", "mapx", "mapy"),
            P("layer", "mapx", "mapy"),
            P("mapx", "mapy"),
            P("mapx", "mapy", None, None),
            P("mapx", "mapy", None),
            P(None, "mapx", ("mapy", "layer")),
            P("mapx", ("mapy", "layer")),
        ),
        out_specs=(P(None, None, "layer", "mapx", "mapy"), P(None, "mapx", ("mapy", "layer"))),
        check_vma=False,
    )
```

```python
import functools

import jax
import jax.numpy as jnp
from jax import lax
from jax.experimental import pallas as pl
from jax.experimental.pallas import tpu as pltpu
from jax.sharding import PartitionSpec as P

F32 = jnp.float32
BF16 = jnp.bfloat16
X, Y, ZV, ZM, R, C = 0, 2, 4, 6, 8, 10


def corner_slot(dx, do):
    return (dx + 1) * 2 + (0 if do < 0 else 1)


def kernel(
    counts, *refs,
):
    inputs, (img_out, hess_out), staged, (img, hess) = refs[:7], refs[7:9], refs[9:16], refs[16:18]
    (
        xs, xh, ys, yh, zh, mh, cs, ch, rs, rh, tr, onehot, lhs, part, got, prior,
        load, store, send, recv, part_send, part_recv, trace_send, trace_recv,
    ) = refs[18:]
    loads = [
        pltpu.make_async_copy(src, dst, load.at[i])
        for i, (src, dst) in enumerate(zip(inputs, staged))
    ]
    vel, visc, fric, own, cell, dirs, stiff = staged
    nx, ny, nl = counts
    no = ny * nl
    nq, depth, rows, cols = vel.shape
    nv = nq * depth
    probes = nq // 2
    mrows, mcols = stiff.shape
    halves = probes // 8
    ix, iy, il = lax.axis_index("mapx"), lax.axis_index("mapy"), lax.axis_index("layer")
    me = iy * nl + il

    def place(at_x, owner):
        return (at_x, lax.div(owner, nl), lax.rem(owner, nl))

    low_x, high_x = ix > 0, ix < nx - 1
    low_y, high_y = iy > 0, iy < ny - 1
    low_l, high_l = il > 0, il < nl - 1
    low_o, high_o = me > 0, me < no - 1

    def has(dx, do):
        good_x = {-1: low_x, 1: high_x}.get(dx)
        good_o = {-1: low_o, 1: high_o}.get(do)
        if good_x is None:
            return good_o
        return good_x if good_o is None else jnp.logical_and(good_x, good_o)

    barrier = pltpu.get_barrier_semaphore()
    for step in range(1, ny):
        pl.semaphore_signal(barrier, inc=1, device_id=(ix, lax.rem(iy + step, ny), il), device_id_type=pl.DeviceIdType.MESH)
    for step in range(1, nl):
        pl.semaphore_signal(barrier, inc=1, device_id=(ix, iy, lax.rem(il + step, nl)), device_id_type=pl.DeviceIdType.MESH)
    greeted = ny - 1 + nl - 1
    for dx in (-1, 0, 1):
        for do in ((-1, 1) if dx == 0 else (-1, 0, 1)):
            near = has(dx, do)
            if dx == 0:
                near = jnp.logical_and(near, il == (0 if do < 0 else nl - 1))
            greeted = greeted + near.astype(jnp.int32)

            @pl.when(near)
            def _(dx=dx, do=do):
                pl.semaphore_signal(
                    barrier, inc=1, device_id=place(ix + dx, me + do),
                    device_id_type=pl.DeviceIdType.MESH,
                )

    for copy in loads:
        copy.start()

    def remote(src, dst, out_sem, in_sem, device):
        return pltpu.make_async_remote_copy(
            src_ref=src, dst_ref=dst, send_sem=out_sem, recv_sem=in_sem,
            device_id=device, device_id_type=pl.DeviceIdType.MESH,
        )

    def pair(kind, src, dst, side, device):
        return remote(src, dst, send.at[kind + side], recv.at[kind + 1 - side], device)

    def x_copy(side):
        return pair(X, xs.at[side], xh.at[1 - side], side, place(ix + 2 * side - 1, me))

    def r_copy(side):
        return pair(R, rs.at[side], rh.at[1 - side], side, place(ix + 2 * side - 1, me))

    def y_copy(side):
        return pair(Y, ys.at[side], yh.at[1 - side], side, (ix, iy + 2 * side - 1, il))

    def z_copy(side):
        z = 0 if side == 0 else depth - 1
        return pair(ZV, vel.at[:, z], zh.at[1 - side], side, (ix, iy, il + 2 * side - 1))

    def m_copy(side):
        z = 0 if side == 0 else depth - 1
        return pair(ZM, visc.at[z], mh.at[1 - side], side, (ix, iy, il + 2 * side - 1))

    def c_copy(dx, do):
        return remote(
            cs.at[0 if do < 0 else 1], ch.at[corner_slot(-dx, -do)],
            send.at[C + corner_slot(dx, do)], recv.at[C + corner_slot(-dx, -do)],
            place(ix + dx, me + do),
        )

    lane = lax.broadcasted_iota(jnp.int32, (rows, cols), 1)
    sub = lax.broadcasted_iota(jnp.int32, (rows, cols), 0)
    zeros = jnp.zeros((rows, cols), F32)

    loads[0].wait()
    loads[1].wait()
    for z in range(depth):
        xs[0, z * nq:(z + 1) * nq, :] = vel[:, z, 0, :]
        xs[1, z * nq:(z + 1) * nq, :] = vel[:, z, rows - 1, :]
    for side, row in ((0, 0), (1, rows - 1)):
        xs[side, nv:nv + 8, :] = jnp.concatenate(
            [visc[z, row:row + 1, :] for z in range(depth)]
            + [jnp.zeros((8 - depth, cols), F32)], 0,
        )

    def put(value, at, packed):
        here = lane == at
        return (
            jnp.where(here, pltpu.roll(value, at, 1), packed[0]),
            jnp.where(here, pltpu.roll(value, at + 1, 1), packed[1]),
        )

    def pack_y(q, packed):
        for z in range(depth):
            packed = put(vel[q, z], z * nq + q, packed)
        return packed

    packed = lax.fori_loop(0, nq, pack_y, (zeros, zeros), unroll=8)
    for z in range(depth):
        packed = put(visc[z], nv + z, packed)
    ys[0], ys[1] = packed

    loads[5].wait()
    loads[6].wait()
    block = [dirs[pl.ds(r, probes, stride=mrows), :] for r in range(mrows)]
    rim = jnp.concatenate([stiff[...], jnp.zeros((8 - mrows, mcols), F32)], 0)
    for side, first in ((0, 0), (1, mrows - 2)):
        for r in range(2):
            rs[side, r * probes:(r + 1) * probes, :] = block[first + r]
        rs[side, 2 * probes:2 * probes + 8, :] = rim
        cs[side, 8:16, :] = rim
    two = lax.div(lane, 2)
    packed = (zeros, zeros)
    for k in range(mrows * halves):
        value = block[k // halves][(k % halves) * 8:(k % halves) * 8 + 8]
        packed = (
            jnp.where(two == k, pltpu.roll(value, 2 * k, 1) if k else value, packed[0]),
            jnp.where(two == k, pltpu.roll(value, 2 * k + 2, 1), packed[1]),
        )
    cs[0, 0:8, :], cs[1, 0:8, :] = packed

    pl.semaphore_wait(barrier, greeted)

    def when_near(near, copy):
        @pl.when(near)
        def _():
            copy().start()

    sides = (0, 1)
    near_x, near_y, near_l = (low_x, high_x), (low_y, high_y), (low_l, high_l)
    corners = [(dx, do) for dx in (-1, 0, 1) for do in (-1, 1)]
    for s in sides:
        when_near(near_x[s], functools.partial(x_copy, s))
        when_near(near_y[s], functools.partial(y_copy, s))
    for s in sides:
        when_near(near_x[s], functools.partial(r_copy, s))
    for dx, do in corners:
        when_near(has(dx, do), functools.partial(c_copy, dx, do))
    for s in sides:
        when_near(near_l[s], functools.partial(m_copy, s))
        when_near(near_l[s], functools.partial(z_copy, s))

    def zero_unless(near, ref, at):
        @pl.when(jnp.logical_not(near))
        def _():
            ref[at] = jnp.zeros(ref.shape[1:], F32)

    for s in sides:
        zero_unless(near_x[s], xh, s)
        zero_unless(near_y[s], yh, s)
        zero_unless(near_l[s], zh, s)
        zero_unless(near_l[s], mh, s)
        zero_unless(near_x[s], rh, s)
    for dx, do in corners:
        zero_unless(has(dx, do), ch, corner_slot(dx, do))

    span = 2 * mcols
    pairs = mrows // 2
    for i in (2, 3, 4):
        loads[i].wait()
    cells = cell[...]
    low = lax.rem(cells, span)
    owners = own[...]
    group = jnp.where(
        lax.rem(owners, nl) == il, lax.div(owners, nl) * pairs + lax.div(cells, span), -1
    )
    number = lax.broadcasted_iota(jnp.int32, (span, cols), 0)
    for x in range(rows):
        onehot[:, x * cols:(x + 1) * cols] = jnp.where(
            number == low[x:x + 1, :], 1.0, 0.0
        ).astype(BF16)

    def arrive(near, copy):
        @pl.when(near)
        def _():
            copy().wait_recv()

    def beside(value, index, halo_rows, halo_lanes):
        down = jnp.where(sub == 0, halo_rows[0], pltpu.roll(value, 1, 0))
        up = jnp.where(sub == rows - 1, halo_rows[1], pltpu.roll(value, rows - 1, 0))
        left = jnp.where(
            lane == 0, pltpu.roll(halo_lanes[0], cols - index, 1), pltpu.roll(value, 1, 1)
        )
        right = jnp.where(
            lane == cols - 1,
            pltpu.roll(halo_lanes[1], cols - 1 - index, 1),
            pltpu.roll(value, cols - 1, 1),
        )
        return down, up, left, right

    def rows_at(index):
        return tuple(
            jnp.broadcast_to(xh[s, pl.ds(index, 1), :], (rows, cols)) for s in sides
        )

    def image_copy(z):
        return pltpu.make_async_copy(img.at[:, z], img_out.at[:, z], store.at[z])

    def plane(z, trace):
        lanes = (yh[0], yh[1])
        here = visc[z]
        around = beside(here, nv + z, rows_at(nv + z), lanes)
        mean = [0.5 * (here + other) for other in around]
        down_z = here + (mh[0] if z == 0 else visc[z - 1])
        up_z = here + (mh[1] if z == depth - 1 else visc[z + 1])
        weights = (
            (mean[0], mean[1], 0.25 * mean[2], 0.25 * mean[3]),
            (0.25 * mean[0], 0.25 * mean[1], mean[2], mean[3]),
        )
        rub = fric[...]

        def probe(p, carry):
            both = None
            for c in range(2):
                q = p * 2 + c
                value = vel[q, z]
                below = zh[0, q] if z == 0 else vel[q, z - 1]
                above = zh[1, q] if z == depth - 1 else vel[q, z + 1]
                index = z * nq + q
                total = up_z * (value - above) + down_z * (value - below)
                for weight, other in zip(
                    weights[c], beside(value, index, rows_at(index), lanes)
                ):
                    total = total + weight * (value - other)
                img[q, z] = total
                both = total if both is None else both + total
            if trace:
                tr[pl.ds(p, rows, stride=probes), :] = rub * both
            return carry

        lax.fori_loop(0, probes, probe, 0, unroll=4)
        image_copy(z).start()

    for s in sides:
        arrive(near_x[s], functools.partial(x_copy, 1 - s))
        arrive(near_y[s], functools.partial(y_copy, 1 - s))

    def smooth():
        for s in sides:
            arrive(near_x[s], functools.partial(r_copy, 1 - s))
        for dx, do in corners:
            arrive(has(dx, do), functools.partial(c_copy, -dx, -do))

        def edge(dx, r):
            left, right = ch[corner_slot(dx, -1), 0:8, :], ch[corner_slot(dx, 1), 0:8, :]
            halfs = []
            for h in range(halves):
                k = 2 * (r * halves + h)
                from_right = pltpu.roll(right, mcols - k, 1) if k else right
                from_left = pltpu.roll(left, mcols - 2 - k, 1)
                halfs.append(
                    jnp.where(lane < 2, from_right, jnp.where(lane >= mcols - 2, from_left, 0.0))
                )
            return jnp.concatenate(halfs, 0)

        wide = {}
        for r in range(2):
            wide[r - 2] = jnp.concatenate(
                [rh[0, r * probes:(r + 1) * probes, :], edge(-1, mrows - 2 + r)], 1
            )
            wide[mrows + r] = jnp.concatenate(
                [rh[1, r * probes:(r + 1) * probes, :], edge(1, r)], 1
            )
        for r in range(mrows):
            wide[r] = jnp.concatenate([dirs[pl.ds(r, probes, stride=mrows), :], edge(0, r)], 1)

        def laplace(field, r):
            return (
                4.0 * field[r] - field[r - 1] - field[r + 1]
                - pltpu.roll(field[r], 1, 1) - pltpu.roll(field[r], 2 * mcols - 1, 1)
            )

        line = lax.broadcasted_iota(jnp.int32, (1, mcols), 1)
        inner = {}
        for r in range(-1, mrows + 1):
            if r < 0:
                soft = rh[0, 2 * probes + mrows - 1:2 * probes + mrows, :]
            elif r == mrows:
                soft = rh[1, 2 * probes:2 * probes + 1, :]
            else:
                soft = stiff[r:r + 1, :]
            outer = jnp.zeros((1, mcols), F32)
            if 0 <= r < mrows:
                outer = jnp.where(
                    line == 0, ch[corner_slot(0, 1), 8 + r:9 + r, :],
                    jnp.where(line == mcols - 1, ch[corner_slot(0, -1), 8 + r:9 + r, :], 0.0),
                )
            inner[r] = jnp.concatenate([soft, outer], 1) * laplace(wide, r)
        for r in range(mrows):
            prior[r * probes:(r + 1) * probes, :] = (
                laplace(inner, r) + 0.1 * wide[r]
            )[:, :mcols]

    def arrive_layers():
        for s in reversed(sides):
            arrive(near_l[s], functools.partial(m_copy, 1 - s))
            arrive(near_l[s], functools.partial(z_copy, 1 - s))

    chunk = min(8, ny)
    tall = 2 * probes

    def trace_copy(layer):
        return remote(
            tr, tr, trace_send.at[layer], trace_recv, (ix, iy, layer)
        )

    def part_copy(to):
        return remote(
            part.at[to], got.at[iy], part_send.at[to], part_recv.at[iy], (ix, to, il)
        )

    @pl.when(il == 0)
    def _():
        plane(0, True)
        for layer in range(1, nl):
            trace_copy(layer).start()

    @pl.when(il != 0)
    def _():
        smooth()
        arrive_layers()
        for z in reversed(range(depth)):
            plane(z, False)
        trace_copy(0).wait_recv()

    coarse, fine = [], []
    for x in range(rows):
        values = tr[x * probes:(x + 1) * probes, :]
        coarse.append(values.astype(BF16).astype(F32))
        fine.append(values - coarse[-1])

    def reduce_chunk(base):
        for g in range(chunk * pairs):
            for x in range(rows):
                mine = group[x:x + 1, :] == base * pairs + g
                lhs[g * tall:(g + 1) * tall, x * cols:(x + 1) * cols] = jnp.concatenate(
                    [jnp.where(mine, coarse[x], 0.0), jnp.where(mine, fine[x], 0.0)], 0
                ).astype(BF16)
        sums = lax.dot_general(
            lhs[...], onehot[...], (((1,), (1,)), ((), ())), preferred_element_type=F32
        )
        for j in range(chunk):
            for h in range(pairs):
                at = (j * pairs + h) * tall
                both = sums[at:at + probes] + sums[at + probes:at + tall]
                for k in range(2):
                    row = (2 * h + k) * probes
                    part[base + j, row:row + probes, :] = both[:, k * mcols:(k + 1) * mcols]

    if ny == chunk:
        reduce_chunk(0)
    else:
        def chunk_step(i, carry):
            reduce_chunk(i * chunk)
            return carry

        lax.fori_loop(0, ny // chunk, chunk_step, 0)
    steps = sorted(range(1, ny), key=lambda step: abs(step - ny // 2))
    for step in steps:
        part_copy(lax.rem(iy + step, ny)).start()

    @pl.when(il == 0)
    def _():
        smooth()
        arrive_layers()
        for z in range(1, depth):
            plane(z, False)

    for step in reversed(steps):
        b = lax.rem(iy + step, ny)
        remote(
            part.at[0], got.at[b], part_send.at[0], part_recv.at[b], (ix, b, il)
        ).wait_recv()
    for r in range(mrows):
        at = slice(r * probes, (r + 1) * probes)
        total = prior[at, :] + part[iy, at, :]
        for step in range(1, ny):
            total = total + got[lax.rem(iy + step, ny), at, :]
        hess[pl.ds(r, probes, stride=mrows), :] = total
    hess_copy = pltpu.make_async_copy(hess, hess_out, store.at[depth])
    hess_copy.start()

    def sent(near, copy):
        @pl.when(near)
        def _():
            copy().wait_send()

    for s in sides:
        for near, copy in (
            (near_x[s], x_copy), (near_y[s], y_copy), (near_l[s], m_copy),
            (near_l[s], z_copy), (near_x[s], r_copy),
        ):
            sent(near, functools.partial(copy, s))
    for dx, do in corners:
        sent(has(dx, do), functools.partial(c_copy, dx, do))
    for step in steps:
        part_copy(lax.rem(iy + step, ny)).wait_send()
    for layer in range(1, nl):
        sent(il == 0, functools.partial(trace_copy, layer))
    for z in range(depth):
        image_copy(z).wait()
    hess_copy.wait()


def deliver_kernel(image, hessian, image_out, hessian_out, image_in, hessian_in, first, second):
    quarter = image.shape[0] // 4
    steps = [(hessian, hessian_in, hessian_out)]
    for i in range(4):
        rows = pl.ds(i * quarter, quarter)
        steps.append((image.at[rows], image_in.at[rows], image_out.at[rows]))
    loads = [
        pltpu.make_async_copy(src, mid, first.at[i]) for i, (src, mid, _) in enumerate(steps)
    ]
    stores = [
        pltpu.make_async_copy(mid, dst, second.at[i]) for i, (_, mid, dst) in enumerate(steps)
    ]
    for copy in loads:
        copy.start()
    for load, store in zip(loads, stores):
        load.wait()
        store.start()
    for copy in stores:
        copy.wait()


def deliver(image, hessian):
    whole = pl.BlockSpec(memory_space=pltpu.HBM)
    return pl.pallas_call(
        deliver_kernel,
        out_shape=tuple(jax.ShapeDtypeStruct(a.shape, a.dtype) for a in (image, hessian)),
        in_specs=[whole, whole],
        out_specs=(whole, whole),
        scratch_shapes=[
            pltpu.VMEM(image.shape, F32),
            pltpu.VMEM(hessian.shape, F32),
            pltpu.SemaphoreType.DMA((5,)),
            pltpu.SemaphoreType.DMA((5,)),
        ],
        compiler_params=pltpu.CompilerParams(vmem_limit_bytes=60 << 20),
        name="deliver",
    )(image, hessian)


def shards(velocity, viscosity, friction, owner, cell, directions, stiffness):
    probes = velocity.shape[0]
    depth, rows, cols = viscosity.shape
    mrows, mcols = stiffness.shape
    counts = tuple(lax.axis_size(axis) for axis in ("mapx", "mapy", "layer"))
    nq = probes * 2
    nv = nq * depth
    chunk = min(8, counts[1])
    whole = pl.BlockSpec(memory_space=pltpu.HBM)
    image, hessian = pl.pallas_call(
        functools.partial(kernel, counts),
        out_shape=(
            jax.ShapeDtypeStruct((nq, depth, rows, cols), F32),
            jax.ShapeDtypeStruct((probes * mrows, mcols), F32),
        ),
        in_specs=[whole] * 7,
        out_specs=(whole, whole),
        scratch_shapes=[
            pltpu.VMEM((nq, depth, rows, cols), F32),
            pltpu.VMEM((depth, rows, cols), F32),
            pltpu.VMEM((rows, cols), F32),
            pltpu.VMEM((rows, cols), jnp.int32),
            pltpu.VMEM((rows, cols), jnp.int32),
            pltpu.VMEM((probes * mrows, mcols), F32),
            pltpu.VMEM((mrows, mcols), F32),
            pltpu.VMEM((nq, depth, rows, cols), F32),
            pltpu.VMEM((probes * mrows, mcols), F32),
            pltpu.VMEM((2, nv + 8, cols), F32),
            pltpu.VMEM((2, nv + 8, cols), F32),
            pltpu.VMEM((2, rows, cols), F32),
            pltpu.VMEM((2, rows, cols), F32),
            pltpu.VMEM((2, nq, rows, cols), F32),
            pltpu.VMEM((2, rows, cols), F32),
            pltpu.VMEM((2, 16, mcols), F32),
            pltpu.VMEM((6, 16, mcols), F32),
            pltpu.VMEM((2, 2 * probes + 8, mcols), F32),
            pltpu.VMEM((2, 2 * probes + 8, mcols), F32),
            pltpu.VMEM((rows * probes, cols), F32),
            pltpu.VMEM((2 * mcols, rows * cols), BF16),
            pltpu.VMEM((chunk * (mrows // 2) * 2 * probes, rows * cols), BF16),
            pltpu.VMEM((counts[1], mrows * probes, mcols), F32),
            pltpu.VMEM((counts[1], mrows * probes, mcols), F32),
            pltpu.VMEM((mrows * probes, mcols), F32),
            pltpu.SemaphoreType.DMA((7,)),
            pltpu.SemaphoreType.DMA((depth + 1,)),
            pltpu.SemaphoreType.DMA((16,)),
            pltpu.SemaphoreType.DMA((16,)),
            pltpu.SemaphoreType.DMA((counts[1],)),
            pltpu.SemaphoreType.DMA((counts[1],)),
            pltpu.SemaphoreType.DMA((counts[2],)),
            pltpu.SemaphoreType.DMA,
        ],
        compiler_params=pltpu.CompilerParams(
            collective_id=0, has_side_effects=True, vmem_limit_bytes=60 << 20
        ),
        name="hessian_action",
    )(
        velocity.reshape(nq, depth, rows, cols),
        viscosity,
        friction,
        owner.reshape(rows, cols),
        cell.reshape(rows, cols),
        directions.reshape(probes * mrows, mcols),
        stiffness,
    )
    image, hessian = deliver(image, hessian)
    return image.reshape(velocity.shape), hessian.reshape(directions.shape)


def solution(mesh):
    return jax.shard_map(
        shards,
        mesh=mesh,
        in_specs=(
            P(None, None, "layer", "mapx", "mapy"),
            P("layer", "mapx", "mapy"),
            P("mapx", "mapy"),
            P("mapx", "mapy", None, None),
            P("mapx", "mapy", None),
            P(None, "mapx", ("mapy", "layer")),
            P("mapx", ("mapy", "layer")),
        ),
        out_specs=(P(None, None, "layer", "mapx", "mapy"), P(None, "mapx", ("mapy", "layer"))),
        check_vma=False,
    )
```
